32 devices in a mesh: blk: 8 (over z, y), rep: 4 (over x, core).
Axes of the slice: x: 2, y: 2, z: 4, core: 2. Of those that a mesh axis runs over, the one named last changes fastest.
Arguments:
- users: bfloat16 [32768, 128], P(('blk', 'rep')), may hold values from -2 to 2
- items: bfloat16 [8192, 128], P('blk'), may hold values from -2 to 2
- ratings: bfloat16 [8, 4, 3, 40, 128, 128], P('blk', 'rep'), may hold values from 0 to 4
- user_tiles: int32 [8, 4, 3, 40], P('blk', 'rep'), may hold values from 0 to 7
- item_tiles: int32 [8, 4, 3, 40], P('blk', 'rep'), may hold values from 0 to 7
- counts: int32 [8, 4, 3], P('blk', 'rep'), may hold values from 5 to 40, as said below
Outputs:
- user_new: bfloat16 [32768, 128], P(('blk', 'rep'))
- item_new: bfloat16 [8192, 128], P('blk')
The draws below stay inside these ranges and needn't reach their ends.
Inputs may be any that keep to these rules, and one draw needn't show every extreme that they name: `counts`: each device and stop has between 5 and 40 live slots, the first ones of its list; some device has all 40 live for some stop.
All inputs are finite; a program needn't handle non-finite values.
Results may differ from the reference program's by a relative error of at most 0.0033.
Values may be sent and summed in bfloat16 or wider, within the bound.
No kernel may reach another device: no remote copies, remote signals or barrier semaphores. Data moves between devices by JAX's collectives and lax.ppermute only.
A program may use at most 64 MiB of HBM per device.

```python
import math
import jax
import jax.numpy as jnp
from jax import lax

K = 128
TILE = 128
USER_DEV = 1024
ITEM_BLK = 1024
STOPS = 3
TILE_SLOTS = 40
USERS = 32768
ITEMS = 8192
N_BLK = 8
N_REP = 4


def draw_counts(key, part):
    grid_shape = (N_BLK, N_REP, STOPS)
    loaded = jax.random.randint(jax.random.fold_in(key, 11), grid_shape, 0, 8) == 0
    baseline = jax.random.randint(jax.random.fold_in(key, 12), grid_shape, max(TILE_SLOTS // 8, 1), TILE_SLOTS // 2 + 1)
    filled = jnp.where(loaded, TILE_SLOTS, baseline).astype(jnp.int32)
    chosen = jax.random.randint(jax.random.fold_in(key, 13), (), 0, N_BLK * N_REP * STOPS)
    flattened = filled.reshape(-1).at[chosen].set(TILE_SLOTS)
    return flattened.reshape(grid_shape).astype(jnp.int32)


def place_ends(result, rng, least, top_value):
    longest = result.shape.index(max(result.shape))
    spots = []
    for shift in (0, 1):
        where = [jax.random.randint(jax.random.fold_in(rng, axis), (), 0, length) for axis, length in enumerate(result.shape)]
        where[longest] = (where[longest] + shift) % result.shape[longest]
        spots.append(tuple(where))
    return result.at[spots[0]].set(least).at[spots[1]].set(top_value)


def shard_levels(stream_key, shape, split, least, top_value):
    factor_of = 1.0
    for position, parts in split:
        steps = jax.random.uniform(jax.random.fold_in(jax.random.fold_in(stream_key, 6), position), (parts,), jnp.float32, least / len(split), top_value / len(split))
        factor_of = factor_of * jnp.repeat(jnp.exp(steps), shape[position] // parts).reshape((-1,) + (1,) * (len(shape) - 1 - position))
    return factor_of


def scatter_about(rng, dims, scale, bound, split=(), held_as=jnp.bfloat16):
    drawn = jax.random.normal(rng, dims, jnp.float32) * scale
    if len(split) > 0:
        drawn = shard_levels(rng, dims, split, -0.22, 0.18) * drawn
    return jnp.clip(drawn, min=-bound, max=bound).astype(held_as)


def setup_inputs(seed: int = 0) -> dict:
    streams_of = jax.random.split(jax.random.key(seed), 7)
    return {
        "users": scatter_about(streams_of[0], (USERS, K), 0.3, 2.0, ((0, 32),)),
        "items": scatter_about(streams_of[1], (ITEMS, K), 0.3, 2.0, ((0, 8),)),
        "ratings": jnp.clip(4.0 * jax.random.uniform(streams_of[2], (N_BLK, N_REP, STOPS, TILE_SLOTS, TILE, TILE), jnp.float32) ** shard_levels(streams_of[2], (N_BLK, N_REP, STOPS, TILE_SLOTS, TILE, TILE), ((0, 8), (1, 4)), -0.2, 0.2), 0.0, 4.0).astype(jnp.bfloat16),
        "user_tiles": place_ends(jax.random.randint(streams_of[3], (N_BLK, N_REP, STOPS, TILE_SLOTS), 0, USER_DEV // TILE), jax.random.fold_in(streams_of[3], 1), 0, (USER_DEV // TILE) - 1).astype(jnp.int32),
        "item_tiles": place_ends(jax.random.randint(streams_of[4], (N_BLK, N_REP, STOPS, TILE_SLOTS), 0, ITEM_BLK // TILE), jax.random.fold_in(streams_of[4], 1), 0, (ITEM_BLK // TILE) - 1).astype(jnp.int32),
        "counts": draw_counts(jax.random.fold_in(streams_of[6], 71), 0),
    }


confidence = 0.5
shrinkage = 0.05
step_gain = 0.3

def slot_terms(user_block, item_block, user_pick, item_pick, rating_tiles, live_count):
    slot_ids = jnp.arange(TILE_SLOTS)
    valid_slots = (slot_ids < live_count).astype(jnp.float32)
    user_rows = user_block[user_pick]
    item_rows = item_block[item_pick]
    predicted = jnp.einsum('gak,gbk->gab', user_rows, item_rows, precision=lax.Precision.HIGHEST)
    rating_vals = rating_tiles.astype(jnp.float32)
    residual = (1.0 + confidence * rating_vals) * (rating_vals - predicted) * valid_slots[:, None, None]
    residual = lax.optimization_barrier(residual.astype(jnp.bfloat16)).astype(jnp.float32)
    user_terms = jnp.einsum('gab,gbk->gak', residual, item_rows, precision=lax.Precision.HIGHEST)
    item_terms = jnp.einsum('gab,gak->gbk', residual, user_rows, precision=lax.Precision.HIGHEST)
    user_grad = jnp.zeros(user_block.shape, jnp.float32).at[user_pick].add(user_terms)
    item_grad = jnp.zeros(item_block.shape, jnp.float32).at[item_pick].add(item_terms)
    return (user_grad, item_grad)

def reference(users, items, ratings, user_tiles, item_tiles, counts):
    user_count = USER_DEV // TILE
    item_count = ITEM_BLK // TILE
    user_blocks = users.astype(jnp.float32).reshape(N_BLK, N_REP, user_count, TILE, K)
    item_blocks = items.astype(jnp.float32).reshape(N_BLK, item_count, TILE, K)

    def column(block_index):
        column_users = user_blocks[block_index]
        grad_user = jnp.zeros((N_REP, user_count, TILE, K), jnp.float32)
        stop_parts = []
        for station in range(STOPS):
            item_block = item_blocks[(block_index + station) % N_BLK]
            user_grad, item_grad = jax.vmap(slot_terms, in_axes=(0, None, 0, 0, 0, 0))(column_users, item_block, user_tiles[block_index, :, station], item_tiles[block_index, :, station], ratings[block_index, :, station], counts[block_index, :, station])
            grad_user = grad_user + user_grad
            stop_parts.append(lax.optimization_barrier(jnp.sum(item_grad, axis=0)))
        return (grad_user, jnp.stack(stop_parts))
    grad_user, item_parts = lax.map(column, jnp.arange(N_BLK, dtype=jnp.int32))
    grad_item = jnp.zeros((N_BLK, item_count, TILE, K), jnp.float32)
    for station in range(STOPS):
        grad_item = grad_item + jnp.roll(item_parts[:, station], station, axis=0)
    rate_user = step_gain / math.sqrt(STOPS * TILE_SLOTS * TILE * TILE / USER_DEV)
    rate_item = step_gain / math.sqrt(N_REP * STOPS * TILE_SLOTS * TILE * TILE / ITEM_BLK)
    users32 = users.astype(jnp.float32)
    items32 = items.astype(jnp.float32)
    user_new = users32 - rate_user * (grad_user.reshape(users.shape) + shrinkage * users32)
    item_new = items32 - rate_item * (grad_item.reshape(items.shape) + shrinkage * items32)
    return (user_new.astype(jnp.bfloat16), item_new.astype(jnp.bfloat16))
```

```python
import functools
import math

import jax
import jax.numpy as jnp
from jax import lax
from jax.experimental import pallas as pl
from jax.experimental.pallas import tpu as pltpu
from jax.sharding import PartitionSpec as P

confidence = 0.5
shrinkage = 0.05
step_gain = 0.3
group = 8
cores = 2

NT = (((1,), (1,)), ((), ()))
NN = (((1,), (0,)), ((), ()))


def mul(a, b, dims):
    return lax.dot_general(a, b, dims, preferred_element_type=jnp.float32)


def tile_rows(index, tile):
    return pl.ds(pl.multiple_of(index * tile, tile), tile)


def stop_kernel(which, first, last, rate, *refs):
    if first:
        counts, user_tiles, item_tiles, users, items, ratings = refs[:6]
        refs = refs[6:]
    else:
        counts, user_tiles, item_tiles, users, items, ratings, grad_in = refs[:7]
        refs = refs[7:]
    user_out, item_out, counts_s, ut_s, it_s, users_v, items_v, rbuf, users_t, total, item_t = refs[:11]
    small, arrive = refs[11:]
    tile = ratings.shape[-1]
    slots = ratings.shape[3]
    n_user = users.shape[0] // tile
    n_item = items.shape[0] // tile
    stop = which(lax.rem(lax.axis_index("rep"), cores))
    copies = [
        pltpu.make_async_copy(counts.at[0, 0], counts_s, small.at[0]),
        pltpu.make_async_copy(user_tiles.at[0], ut_s, small.at[1]),
        pltpu.make_async_copy(item_tiles.at[0], it_s, small.at[2]),
        pltpu.make_async_copy(users, users_v, small.at[3]),
        pltpu.make_async_copy(items, items_v, small.at[4]),
    ]
    if not first:
        copies.append(pltpu.make_async_copy(grad_in, total, small.at[5]))
    for copy in copies:
        copy.start()
    copies[0].wait()
    live = counts_s[stop]
    groups = lax.div(live + group - 1, group)

    def tiles_copy(g):
        rows = pl.ds(g * group, group)
        return pltpu.make_async_copy(ratings.at[0, 0, stop, rows], rbuf.at[rows], arrive.at[g])

    def start_copy(g, carry):
        tiles_copy(g).start()
        return carry

    lax.fori_loop(0, groups, start_copy, 0)
    item_t[...] = jnp.zeros_like(item_t)
    if first:
        total[...] = jnp.zeros_like(total)
    for copy in copies[1:]:
        copy.wait()
    for t in range(n_user):
        users_t[t] = users_v[pl.ds(t * tile, tile)].T

    def step(g, carry):
        tiles_copy(g).wait()
        slots_now = []
        for k in range(group):
            s = g * group + k
            u_index = ut_s[stop, 0, s]
            i_index = it_s[stop, 0, s]
            u = users_v[tile_rows(u_index, tile)]
            v = items_v[tile_rows(i_index, tile)]
            r = rbuf[s].astype(jnp.float32)
            e = (1.0 + confidence * r) * (r - mul(u, v, NT))
            e = jnp.where(s < live, e, 0.0).astype(jnp.bfloat16)
            slots_now.append((u_index, i_index, v, e))
        terms = [(a, b, mul(e, v, NN), mul(users_t[a], e, NN)) for a, b, v, e in slots_now]
        for a, b, to_user, to_item in terms:
            total[tile_rows(a, tile)] += to_user
            item_t[b] += to_item
        return carry

    lax.fori_loop(0, groups, step, 0)
    for t in range(n_item):
        item_out[pl.ds(t * tile, tile)] = item_t[t].T
    if last:
        u32 = users_v[...].astype(jnp.float32)
        user_out[...] = (u32 - rate * (total[...] + shrinkage * u32)).astype(user_out.dtype)
    else:
        user_out[...] = total[...]


def meet(which, arrays, grad_in=None, last=False, rate=0.0):
    counts, user_tiles, item_tiles, users, items, ratings = arrays
    first = grad_in is None
    tile, slots, stops = ratings.shape[-1], ratings.shape[3], ratings.shape[2]
    rank = users.shape[1]
    anywhere = pl.BlockSpec(memory_space=pltpu.HBM)
    vmem = pl.BlockSpec(memory_space=pltpu.VMEM)
    operands = list(arrays) + ([] if first else [grad_in])
    return pl.pallas_call(
        functools.partial(stop_kernel, which, first, last, rate),
        out_shape=(
            jax.ShapeDtypeStruct(users.shape, users.dtype if last else jnp.float32),
            jax.ShapeDtypeStruct(items.shape, jnp.float32),
        ),
        in_specs=[anywhere] * len(operands),
        out_specs=(vmem, vmem),
        scratch_shapes=[
            pltpu.SMEM((stops,), jnp.int32),
            pltpu.SMEM((stops, 1, slots), jnp.int32),
            pltpu.SMEM((stops, 1, slots), jnp.int32),
            pltpu.VMEM(users.shape, users.dtype),
            pltpu.VMEM(items.shape, items.dtype),
            pltpu.VMEM((slots, tile, tile), ratings.dtype),
            pltpu.VMEM((users.shape[0] // tile, rank, tile), users.dtype),
            pltpu.VMEM(users.shape, jnp.float32),
            pltpu.VMEM((items.shape[0] // tile, rank, tile), jnp.float32),
            pltpu.SemaphoreType.DMA((6,)),
            pltpu.SemaphoreType.DMA((slots // group,)),
        ],
        compiler_params=pltpu.CompilerParams(vmem_limit_bytes=16 * 2**20),
        cost_estimate=pl.CostEstimate(flops=10**10, bytes_accessed=8 * 10**6, transcendentals=0),
    )(*operands)


def joint(block, target):
    n_blk, n_rep = lax.axis_size("blk"), lax.axis_size("rep")
    route = []
    for b in range(n_blk):
        for r in range(n_rep):
            to_b, to_r = target(b, r)
            route.append((b * n_rep + r, (to_b % n_blk) * n_rep + to_r))
    return lax.ppermute(block, ("blk", "rep"), route)


def swap(block, bit):
    return lax.ppermute(block, "rep", [(r, r ^ bit) for r in range(lax.axis_size("rep"))])


def on_device(users, items, ratings, user_tiles, item_tiles, counts):
    tile, slots, stops = ratings.shape[-1], ratings.shape[3], ratings.shape[2]
    n_rep = lax.axis_size("rep")
    core = lax.rem(lax.axis_index("rep"), cores)
    slot_cells = stops * slots * tile * tile
    rate_user = step_gain / math.sqrt(slot_cells / users.shape[0])
    rate_item = step_gain / math.sqrt(n_rep * slot_cells / items.shape[0])
    bound = cores * slots * tile * 2.0 * 3.0 * (4.0 + 4.0 * users.shape[1])
    scale = 2.0 ** math.floor(math.log2(60000.0 / bound))

    user_tiles, item_tiles = (a.transpose(0, 2, 1, 3) for a in (user_tiles, item_tiles))

    fixed = [pltpu.with_memory_space_constraint(a, pltpu.HBM) for a in (counts, user_tiles, item_tiles, users, ratings)]

    def arrays(block):
        return (*fixed[:4], block, fixed[4])

    near = joint(items, lambda b, r: (b - 2 + r % cores, r))
    grad_user, own = meet(lambda c: c * 0, arrays(pltpu.with_memory_space_constraint(items, pltpu.HBM)))
    far = swap(near, 1)
    grad_user, given = meet(lambda c: 2 - c, arrays(near), grad_user)
    taken = swap(given, 1)
    user_new, kept = meet(lambda c: 1 + c, arrays(far), grad_user, True, rate_user)
    sent = ((kept + taken) * scale).astype(jnp.float16)
    come = joint(sent, lambda b, r: (b + 1 + r % cores, r)).astype(jnp.float32) * (1.0 / scale)
    column = come + own
    half = items.shape[0] // cores
    mine = lax.dynamic_slice_in_dim(column, core * half, half)
    theirs = lax.dynamic_slice_in_dim(column, (1 - core) * half, half)
    chip = mine + swap(theirs, 1)
    bit = cores
    while bit < n_rep:
        coded = lax.optimization_barrier((chip * scale).astype(jnp.float16))
        both = coded.astype(jnp.float32) + swap(coded, bit).astype(jnp.float32)
        chip = both * (1.0 / scale)
        bit *= 2
    items32 = lax.dynamic_slice_in_dim(items, core * half, half).astype(jnp.float32)
    new_half = (items32 - rate_item * (chip + shrinkage * items32)).astype(items.dtype)
    other_half = swap(new_half, 1)
    low = jnp.where(core == 0, new_half, other_half)
    high = jnp.where(core == 0, other_half, new_half)
    return user_new, jnp.concatenate([low, high])


def solution(mesh):
    return jax.shard_map(
        on_device,
        mesh=mesh,
        in_specs=(
            P(("blk", "rep"), None),
            P("blk", None),
            P("blk", "rep", None, None, None, None),
            P("blk", "rep", None, None),
            P("blk", "rep", None, None),
            P("blk", "rep", None),
        ),
        out_specs=(P(("blk", "rep"), None), P("blk", None)),
        check_vma=False,
    )
```

```python
import functools
import math

import jax
import jax.numpy as jnp
from jax import lax
from jax.experimental import pallas as pl
from jax.experimental.pallas import tpu as pltpu
from jax.sharding import PartitionSpec as P

confidence = 0.5
shrinkage = 0.05
step_gain = 0.3
chunk = 8
group = 8
cores = 2
f32, bf16, f16 = jnp.float32, jnp.bfloat16, jnp.float16

NT = (((1,), (1,)), ((), ()))
NN = (((1,), (0,)), ((), ()))
anywhere = pl.BlockSpec(memory_space=pl.ANY)
vmem = pl.BlockSpec(memory_space=pltpu.VMEM)


def mul(a, b, dims):
    return lax.dot_general(a, b, dims, preferred_element_type=f32)


def tile_rows(index, tile):
    return pl.ds(pl.multiple_of(index * tile, tile), tile)


def near_stop(core):
    return 2 - core


def far_stop(core):
    return 1 + core


def steps(live, size):
    return lax.div(live + size - 1, size)


def run_slots(live, stop, ut_s, it_s, users, users_t, block, tiles, total, item_t):
    tile = tiles.shape[-1]

    def step(g, carry):
        slots_now = []
        for k in range(group):
            s = g * group + k
            listed = jnp.minimum(s, ut_s.shape[-1] - 1)
            u_index = ut_s[stop, 0, listed]
            i_index = it_s[stop, 0, listed]
            u = users[tile_rows(u_index, tile)]
            v = block[tile_rows(i_index, tile)]
            r = tiles[s].astype(f32)
            e = (1.0 + confidence * r) * (r - mul(u, v, NT))
            e = jnp.where(s < live, e, 0.0).astype(bf16)
            slots_now.append((u_index, i_index, v, e))
        terms = [(a, b, mul(e, v, NN), mul(users_t[a], e, NN)) for a, b, v, e in slots_now]
        for a, b, to_user, to_item in terms:
            total[tile_rows(a, tile)] += to_user
            item_t[b] += to_item
        return carry

    lax.fori_loop(0, steps(live, group), step, 0)


class Tiles:
    def __init__(self, ratings, stop, counts, place, sems):
        self.ratings, self.stop, self.place, self.sems = ratings, stop, place, sems
        self.count = steps(counts[stop], chunk)

    def copy(self, g):
        rows = pl.ds(g * chunk, chunk)
        return pltpu.make_async_copy(self.ratings.at[0, 0, self.stop, rows], self.place.at[rows], self.sems.at[g])

    def start(self):
        def begin(g, carry):
            self.copy(g).start()
            return carry

        lax.fori_loop(0, self.count, begin, 0)

    def wait(self):
        def finish(g, carry):
            self.copy(g).wait()
            return carry

        lax.fori_loop(0, self.count, finish, 0)


def own_kernel(
    counts, user_tiles, item_tiles, users, items, ratings,
    total, own_t, near_r, users_v, users_t, counts_v, ut_v, it_v,
    counts_s, ut_s, it_s, items_v, own_r, small, arrive,
):
    tile = ratings.shape[-1]
    core = lax.rem(lax.axis_index("rep"), cores)
    lists = [
        pltpu.make_async_copy(counts.at[0, 0], counts_s, small.at[0]),
        pltpu.make_async_copy(user_tiles.at[0], ut_s, small.at[1]),
        pltpu.make_async_copy(item_tiles.at[0], it_s, small.at[2]),
    ]
    blocks = [
        pltpu.make_async_copy(users, users_v, small.at[3]),
        pltpu.make_async_copy(items, items_v, small.at[4]),
        pltpu.make_async_copy(counts, counts_v, small.at[5]),
        pltpu.make_async_copy(user_tiles, ut_v, small.at[6]),
        pltpu.make_async_copy(item_tiles, it_v, small.at[7]),
    ]
    for copy in lists + blocks:
        copy.start()
    lists[0].wait()
    plans = [
        Tiles(ratings, 0, counts_s, own_r, arrive.at[0]),
        Tiles(ratings, near_stop(core), counts_s, near_r, arrive.at[1]),
    ]
    for plan in plans:
        plan.start()
    total[...] = jnp.zeros_like(total)
    own_t[...] = jnp.zeros_like(own_t)
    for copy in lists[1:] + blocks:
        copy.wait()
    for t in range(users_t.shape[0]):
        users_t[t] = users_v[pl.ds(t * tile, tile)].T
    plans[0].wait()
    run_slots(counts_s[0], 0, ut_s, it_s, users_v, users_t, items_v, own_r, total, own_t)
    plans[1].wait()


def own_call(counts, user_tiles, item_tiles, users, items, ratings):
    tile, slots, stops, rank = ratings.shape[-1], ratings.shape[3], ratings.shape[2], users.shape[1]
    n_user, n_item = users.shape[0] // tile, items.shape[0] // tile
    some_tiles = (-(-slots // group) * group, tile, tile)
    shape = jax.ShapeDtypeStruct
    return pl.pallas_call(
        own_kernel,
        out_shape=(
            shape(users.shape, f32),
            shape((n_item, rank, tile), f32),
            shape(some_tiles, ratings.dtype),
            shape(users.shape, users.dtype),
            shape((n_user, rank, tile), users.dtype),
            shape(counts.shape, counts.dtype),
            shape(user_tiles.shape, user_tiles.dtype),
            shape(item_tiles.shape, item_tiles.dtype),
        ),
        in_specs=[anywhere] * 6,
        out_specs=[vmem] * 8,
        scratch_shapes=[
            pltpu.SMEM((stops,), jnp.int32),
            pltpu.SMEM((stops, 1, slots), jnp.int32),
            pltpu.SMEM((stops, 1, slots), jnp.int32),
            pltpu.VMEM(items.shape, items.dtype),
            pltpu.VMEM(some_tiles, ratings.dtype),
            pltpu.SemaphoreType.DMA((8,)),
            pltpu.SemaphoreType.DMA((2, slots // chunk)),
        ],
        compiler_params=pltpu.CompilerParams(vmem_limit_bytes=8 * 2**20),
        cost_estimate=pl.CostEstimate(flops=10**10, bytes_accessed=8 * 10**6, transcendentals=0),
    )(*[pltpu.with_memory_space_constraint(a, pltpu.HBM) for a in (counts, user_tiles, item_tiles, users, items, ratings)])


def stop_kernel(which, following, *refs):
    counts_v, ut_v, it_v, users, users_t, block, tiles = refs[:7]
    refs = refs[8:]
    if following is not None:
        ratings, total, item_t, tiles_next, counts_s, ut_s, it_s, small, arrive = refs
    else:
        total, item_t, counts_s, ut_s, it_s, small = refs
    lists = [
        pltpu.make_async_copy(counts_v.at[0, 0], counts_s, small.at[0]),
        pltpu.make_async_copy(ut_v.at[0], ut_s, small.at[1]),
        pltpu.make_async_copy(it_v.at[0], it_s, small.at[2]),
    ]
    for copy in lists:
        copy.start()
    item_t[...] = jnp.zeros_like(item_t)
    for copy in lists:
        copy.wait()
    core = lax.rem(lax.axis_index("rep"), cores)
    if following is not None:
        plan = Tiles(ratings, following(core), counts_s, tiles_next, arrive)
        plan.start()
    stop = which(core)
    run_slots(counts_s[stop], stop, ut_s, it_s, users, users_t, block, tiles, total, item_t)
    if following is not None:
        plan.wait()


def stop_call(which, lists, users, users_t, block, tiles, total, following=None, ratings=None):
    slots, tile = lists[1].shape[-1], tiles.shape[-1]
    stops = lists[0].shape[-1]
    operands = [*lists, users, users_t, block, tiles, total]
    out_shape = [
        jax.ShapeDtypeStruct(total.shape, f32),
        jax.ShapeDtypeStruct((block.shape[0] // tile, block.shape[1], tile), f32),
    ]
    scratch = [
        pltpu.SMEM((stops,), jnp.int32),
        pltpu.SMEM((stops, 1, slots), jnp.int32),
        pltpu.SMEM((stops, 1, slots), jnp.int32),
        pltpu.SemaphoreType.DMA((3,)),
    ]
    in_specs = [vmem] * len(operands)
    aliases = {len(operands) - 1: 0}
    if following is not None:
        operands.append(pltpu.with_memory_space_constraint(ratings, pltpu.HBM))
        in_specs.append(anywhere)
        out_shape.append(jax.ShapeDtypeStruct(tiles.shape, tiles.dtype))
        scratch.append(pltpu.SemaphoreType.DMA((slots // chunk,)))
    return pl.pallas_call(
        functools.partial(stop_kernel, which, following),
        out_shape=out_shape,
        in_specs=in_specs,
        out_specs=[vmem] * len(out_shape),
        input_output_aliases=aliases,
        scratch_shapes=scratch,
        compiler_params=pltpu.CompilerParams(vmem_limit_bytes=4 * 2**20),
        cost_estimate=pl.CostEstimate(flops=10**10, bytes_accessed=8 * 10**6, transcendentals=0),
    )(*operands)


def joint(block, target):
    n_blk, n_rep = lax.axis_size("blk"), lax.axis_size("rep")
    route = []
    for b in range(n_blk):
        for r in range(n_rep):
            to_b, to_r = target(b, r)
            route.append((b * n_rep + r, (to_b % n_blk) * n_rep + to_r))
    return lax.ppermute(block, ("blk", "rep"), route)


def swap(block, bit):
    return lax.ppermute(block, "rep", [(r, r ^ bit) for r in range(lax.axis_size("rep"))])


def on_device(users, items, ratings, user_tiles, item_tiles, counts):
    tile, slots, stops = ratings.shape[-1], ratings.shape[3], ratings.shape[2]
    n_rep = lax.axis_size("rep")
    core = lax.rem(lax.axis_index("rep"), cores)
    slot_cells = stops * slots * tile * tile
    rate_user = step_gain / math.sqrt(slot_cells / users.shape[0])
    rate_item = step_gain / math.sqrt(n_rep * slot_cells / items.shape[0])
    bound = cores * slots * tile * 2.0 * 3.0 * (4.0 + 4.0 * users.shape[1])
    scale = 2.0 ** math.floor(math.log2(60000.0 / bound))

    near = joint(items, lambda b, r: (b - near_stop(r % cores), r))
    user_tiles, item_tiles = (a.transpose(0, 2, 1, 3) for a in (user_tiles, item_tiles))
    total, own, near_r, users_v, users_t, *lists = own_call(
        counts, user_tiles, item_tiles, users, items, ratings
    )
    far = swap(near, 1)
    total, given, far_r = stop_call(near_stop, lists, users_v, users_t, near, near_r, total, far_stop, ratings)
    taken = swap(given, 1)
    total, kept = stop_call(far_stop, lists, users_v, users_t, far, far_r, total)
    users32 = users_v.astype(f32)
    user_new = (users32 - rate_user * (total + shrinkage * users32)).astype(users.dtype)
    both = kept + taken
    half = both.shape[0] // cores

    def half_of(array, c):
        return lax.dynamic_slice_in_dim(array, c * half, half)

    straight = joint((half_of(both, core) * scale).astype(f16), lambda b, r: (b + far_stop(r % cores), r))
    across = joint((half_of(both, 1 - core) * scale).astype(f16), lambda b, r: (b + far_stop(r % cores), r ^ 1))
    own_half = half_of(own, core) + swap(half_of(own, 1 - core), 1)
    chip = own_half + (straight.astype(f32) + across.astype(f32)) * (1.0 / scale)
    bit = cores
    while bit < n_rep:
        coded = lax.optimization_barrier((chip * scale).astype(f16))
        chip = (coded.astype(f32) + swap(coded, bit).astype(f32)) * (1.0 / scale)
        bit *= 2
    chip = chip.transpose(0, 2, 1).reshape(-1, users.shape[1])
    rows = items.shape[0] // cores
    items32 = lax.dynamic_slice_in_dim(items, core * rows, rows).astype(f32)
    new_half = (items32 - rate_item * (chip + shrinkage * items32)).astype(items.dtype)
    other_half = swap(new_half, 1)
    low = jnp.where(core == 0, new_half, other_half)
    high = jnp.where(core == 0, other_half, new_half)
    return user_new, jnp.concatenate([low, high])


def solution(mesh):
    return jax.shard_map(
        on_device,
        mesh=mesh,
        in_specs=(
            P(("blk", "rep"), None),
            P("blk", None),
            P("blk", "rep", None, None, None, None),
            P("blk", "rep", None, None),
            P("blk", "rep", None, None),
            P("blk", "rep", None),
        ),
        out_specs=(P(("blk", "rep"), None), P("blk", None)),
        check_vma=False,
    )
```

```python
import functools
import math

import jax
import jax.numpy as jnp
from jax import lax
from jax.experimental import pallas as pl
from jax.experimental.pallas import tpu as pltpu
from jax.sharding import PartitionSpec as P

confidence = 0.5
shrinkage = 0.05
step_gain = 0.3
chunk = 8
group = 20
cores = 2
f32, bf16, f16 = jnp.float32, jnp.bfloat16, jnp.float16

NT = (((1,), (1,)), ((), ()))
NN = (((1,), (0,)), ((), ()))
anywhere = pl.BlockSpec(memory_space=pl.ANY)
vmem = pl.BlockSpec(memory_space=pltpu.VMEM)


def mul(a, b, dims):
    return lax.dot_general(a, b, dims, preferred_element_type=f32)


def tile_rows(index, tile):
    return pl.ds(pl.multiple_of(index * tile, tile), tile)


def near_stop(core):
    return 2 - core


def far_stop(core):
    return 1 + core


def steps(live, size):
    return lax.div(live + size - 1, size)


def run_slots(live, stop, ut_s, it_s, users, users_t, block, tiles, total, item_t):
    tile = tiles.shape[-1]

    def step(g, carry):
        slots_now = []
        for k in range(group):
            s = g * group + k
            listed = jnp.minimum(s, ut_s.shape[-1] - 1)
            u_index = ut_s[stop, 0, listed]
            i_index = it_s[stop, 0, listed]
            u = users[tile_rows(u_index, tile)]
            v = block[tile_rows(i_index, tile)]
            r = tiles[s].astype(f32)
            e = (1.0 + confidence * r) * (r - mul(u, v, NT))
            e = jnp.where(s < live, e, 0.0).astype(bf16)
            slots_now.append((u_index, i_index, v, e))
        terms = [(a, b, mul(e, v, NN), mul(users_t[a], e, NN)) for a, b, v, e in slots_now]
        for a, b, to_user, to_item in terms:
            total[tile_rows(a, tile)] += to_user
            item_t[b] += to_item
        return carry

    lax.fori_loop(0, steps(live, group), step, 0)


class Tiles:
    def __init__(self, ratings, stop, counts, place, sems):
        self.ratings, self.stop, self.place, self.sems = ratings, stop, place, sems
        self.count = steps(counts[stop], chunk)

    def copy(self, g):
        rows = pl.ds(g * chunk, chunk)
        return pltpu.make_async_copy(self.ratings.at[0, 0, self.stop, rows], self.place.at[rows], self.sems.at[g])

    def start(self):
        def begin(g, carry):
            self.copy(g).start()
            return carry

        lax.fori_loop(0, self.count, begin, 0)

    def wait(self):
        def finish(g, carry):
            self.copy(g).wait()
            return carry

        lax.fori_loop(0, self.count, finish, 0)


def own_kernel(
    counts, user_tiles, item_tiles, users, items, ratings,
    total, own_t, near_r, users_v, users_t, counts_v, ut_v, it_v,
    counts_s, ut_s, it_s, items_v, own_r, small, arrive,
):
    tile = ratings.shape[-1]
    core = lax.rem(lax.axis_index("rep"), cores)
    lists = [
        pltpu.make_async_copy(counts.at[0, 0], counts_s, small.at[0]),
        pltpu.make_async_copy(user_tiles.at[0], ut_s, small.at[1]),
        pltpu.make_async_copy(item_tiles.at[0], it_s, small.at[2]),
    ]
    blocks = [
        pltpu.make_async_copy(users, users_v, small.at[3]),
        pltpu.make_async_copy(items, items_v, small.at[4]),
        pltpu.make_async_copy(counts, counts_v, small.at[5]),
        pltpu.make_async_copy(user_tiles, ut_v, small.at[6]),
        pltpu.make_async_copy(item_tiles, it_v, small.at[7]),
    ]
    for copy in lists + blocks:
        copy.start()
    lists[0].wait()
    plans = [
        Tiles(ratings, 0, counts_s, own_r, arrive.at[0]),
        Tiles(ratings, near_stop(core), counts_s, near_r, arrive.at[1]),
    ]
    for plan in plans:
        plan.start()
    total[...] = jnp.zeros_like(total)
    own_t[...] = jnp.zeros_like(own_t)
    for copy in lists[1:] + blocks:
        copy.wait()
    for t in range(users_t.shape[0]):
        users_t[t] = users_v[pl.ds(t * tile, tile)].T
    plans[0].wait()
    run_slots(counts_s[0], 0, ut_s, it_s, users_v, users_t, items_v, own_r, total, own_t)
    plans[1].wait()


def own_call(counts, user_tiles, item_tiles, users, items, ratings):
    tile, slots, stops, rank = ratings.shape[-1], ratings.shape[3], ratings.shape[2], users.shape[1]
    n_user, n_item = users.shape[0] // tile, items.shape[0] // tile
    some_tiles = (-(-slots // group) * group, tile, tile)
    shape = jax.ShapeDtypeStruct
    return pl.pallas_call(
        own_kernel,
        out_shape=(
            shape(users.shape, f32),
            shape((n_item, rank, tile), f32),
            shape(some_tiles, ratings.dtype),
            shape(users.shape, users.dtype),
            shape((n_user, rank, tile), users.dtype),
            shape(counts.shape, counts.dtype),
            shape(user_tiles.shape, user_tiles.dtype),
            shape(item_tiles.shape, item_tiles.dtype),
        ),
        in_specs=[anywhere] * 6,
        out_specs=[vmem] * 8,
        scratch_shapes=[
            pltpu.SMEM((stops,), jnp.int32),
            pltpu.SMEM((stops, 1, slots), jnp.int32),
            pltpu.SMEM((stops, 1, slots), jnp.int32),
            pltpu.VMEM(items.shape, items.dtype),
            pltpu.VMEM(some_tiles, ratings.dtype),
            pltpu.SemaphoreType.DMA((8,)),
            pltpu.SemaphoreType.DMA((2, slots // chunk)),
        ],
        compiler_params=pltpu.CompilerParams(vmem_limit_bytes=8 * 2**20),
        cost_estimate=pl.CostEstimate(flops=10**10, bytes_accessed=8 * 10**6, transcendentals=0),
    )(*[pltpu.with_memory_space_constraint(a, pltpu.HBM) for a in (counts, user_tiles, item_tiles, users, items, ratings)])


def stop_kernel(which, following, *refs):
    counts_v, ut_v, it_v, users, users_t, block, tiles = refs[:7]
    refs = refs[8:]
    if following is not None:
        ratings, total, item_t, tiles_next, counts_s, ut_s, it_s, small, arrive = refs
    else:
        total, item_t, counts_s, ut_s, it_s, small = refs
    lists = [
        pltpu.make_async_copy(counts_v.at[0, 0], counts_s, small.at[0]),
        pltpu.make_async_copy(ut_v.at[0], ut_s, small.at[1]),
        pltpu.make_async_copy(it_v.at[0], it_s, small.at[2]),
    ]
    for copy in lists:
        copy.start()
    item_t[...] = jnp.zeros_like(item_t)
    for copy in lists:
        copy.wait()
    core = lax.rem(lax.axis_index("rep"), cores)
    if following is not None:
        plan = Tiles(ratings, following(core), counts_s, tiles_next, arrive)
        plan.start()
    stop = which(core)
    run_slots(counts_s[stop], stop, ut_s, it_s, users, users_t, block, tiles, total, item_t)
    if following is not None:
        plan.wait()


def stop_call(which, lists, users, users_t, block, tiles, total, following=None, ratings=None):
    slots, tile = lists[1].shape[-1], tiles.shape[-1]
    stops = lists[0].shape[-1]
    operands = [*lists, users, users_t, block, tiles, total]
    out_shape = [
        jax.ShapeDtypeStruct(total.shape, f32),
        jax.ShapeDtypeStruct((block.shape[0] // tile, block.shape[1], tile), f32),
    ]
    scratch = [
        pltpu.SMEM((stops,), jnp.int32),
        pltpu.SMEM((stops, 1, slots), jnp.int32),
        pltpu.SMEM((stops, 1, slots), jnp.int32),
        pltpu.SemaphoreType.DMA((3,)),
    ]
    in_specs = [vmem] * len(operands)
    aliases = {len(operands) - 1: 0}
    if following is not None:
        operands.append(pltpu.with_memory_space_constraint(ratings, pltpu.HBM))
        in_specs.append(anywhere)
        out_shape.append(jax.ShapeDtypeStruct(tiles.shape, tiles.dtype))
        scratch.append(pltpu.SemaphoreType.DMA((slots // chunk,)))
    return pl.pallas_call(
        functools.partial(stop_kernel, which, following),
        out_shape=out_shape,
        in_specs=in_specs,
        out_specs=[vmem] * len(out_shape),
        input_output_aliases=aliases,
        scratch_shapes=scratch,
        compiler_params=pltpu.CompilerParams(vmem_limit_bytes=4 * 2**20),
        cost_estimate=pl.CostEstimate(flops=10**10, bytes_accessed=8 * 10**6, transcendentals=0),
    )(*operands)


def joint(block, target):
    n_blk, n_rep = lax.axis_size("blk"), lax.axis_size("rep")
    route = []
    for b in range(n_blk):
        for r in range(n_rep):
            to_b, to_r = target(b, r)
            route.append((b * n_rep + r, (to_b % n_blk) * n_rep + to_r))
    return lax.ppermute(block, ("blk", "rep"), route)


def swap(block, bit):
    return lax.ppermute(block, "rep", [(r, r ^ bit) for r in range(lax.axis_size("rep"))])


def on_device(users, items, ratings, user_tiles, item_tiles, counts):
    tile, slots, stops = ratings.shape[-1], ratings.shape[3], ratings.shape[2]
    n_rep = lax.axis_size("rep")
    core = lax.rem(lax.axis_index("rep"), cores)
    slot_cells = stops * slots * tile * tile
    rate_user = step_gain / math.sqrt(slot_cells / users.shape[0])
    rate_item = step_gain / math.sqrt(n_rep * slot_cells / items.shape[0])
    bound = cores * slots * tile * 2.0 * 3.0 * (4.0 + 4.0 * users.shape[1])
    scale = 2.0 ** math.floor(math.log2(60000.0 / bound))

    near = joint(items, lambda b, r: (b - near_stop(r % cores), r))
    user_tiles, item_tiles = (a.transpose(0, 2, 1, 3) for a in (user_tiles, item_tiles))
    total, own, near_r, users_v, users_t, *lists = own_call(
        counts, user_tiles, item_tiles, users, items, ratings
    )
    far = swap(near, 1)
    total, given, far_r = stop_call(near_stop, lists, users_v, users_t, near, near_r, total, far_stop, ratings)
    taken = swap(given, 1)
    total, kept = stop_call(far_stop, lists, users_v, users_t, far, far_r, total)
    users32 = users_v.astype(f32)
    user_new = (users32 - rate_user * (total + shrinkage * users32)).astype(users.dtype)
    both = kept + taken
    half = both.shape[0] // cores

    def half_of(array, c):
        return lax.dynamic_slice_in_dim(array, c * half, half)

    straight = joint((half_of(both, core) * scale).astype(f16), lambda b, r: (b + far_stop(r % cores), r))
    across = joint((half_of(both, 1 - core) * scale).astype(f16), lambda b, r: (b + far_stop(r % cores), r ^ 1))
    own_half = half_of(own, core) + swap(half_of(own, 1 - core), 1)
    chip = own_half + (straight.astype(f32) + across.astype(f32)) * (1.0 / scale)
    bit = cores
    while bit < n_rep:
        coded = lax.optimization_barrier((chip * scale).astype(f16))
        chip = (coded.astype(f32) + swap(coded, bit).astype(f32)) * (1.0 / scale)
        bit *= 2
    chip = chip.transpose(0, 2, 1).reshape(-1, users.shape[1])
    rows = items.shape[0] // cores
    items32 = lax.dynamic_slice_in_dim(items, core * rows, rows).astype(f32)
    new_half = (items32 - rate_item * (chip + shrinkage * items32)).astype(items.dtype)
    other_half = swap(new_half, 1)
    low = jnp.where(core == 0, new_half, other_half)
    high = jnp.where(core == 0, other_half, new_half)
    return user_new, jnp.concatenate([low, high])


def solution(mesh):
    return jax.shard_map(
        on_device,
        mesh=mesh,
        in_specs=(
            P(("blk", "rep"), None),
            P("blk", None),
            P("blk", "rep", None, None, None, None),
            P("blk", "rep", None, None),
            P("blk", "rep", None, None),
            P("blk", "rep", None),
        ),
        out_specs=(P(("blk", "rep"), None), P("blk", None)),
        check_vma=False,
    )
```

```python
import functools
import math

import jax
import jax.numpy as jnp
from jax import lax
from jax.experimental import pallas as pl
from jax.experimental.pallas import tpu as pltpu
from jax.sharding import PartitionSpec as P

confidence = 0.5
shrinkage = 0.05
step_gain = 0.3
chunk = 8
group = 20
rests = (8, 12, 16)
cores = 2
f32, bf16, f16 = jnp.float32, jnp.bfloat16, jnp.float16

NT = (((1,), (1,)), ((), ()))
NN = (((1,), (0,)), ((), ()))
anywhere = pl.BlockSpec(memory_space=pl.ANY)
vmem = pl.BlockSpec(memory_space=pltpu.VMEM)


def mul(a, b, dims):
    return lax.dot_general(a, b, dims, preferred_element_type=f32)


def tile_rows(index, tile):
    return pl.ds(pl.multiple_of(index * tile, tile), tile)


def near_stop(core):
    return 2 - core


def far_stop(core):
    return 1 + core


def steps(live, size):
    return (live + size - 1) // size if isinstance(live, int) else lax.div(live + size - 1, size)


def run_slots(live, stop, ut_s, it_s, users, users_t, block, tiles, total, item_t):
    tile = tiles.shape[-1]

    def work(first, size):
        slots_now = []
        for k in range(size):
            s = first + k
            listed = jnp.minimum(s, ut_s.shape[-1] - 1)
            u_index = ut_s[stop, 0, listed]
            i_index = it_s[stop, 0, listed]
            u = users[tile_rows(u_index, tile)]
            v = block[tile_rows(i_index, tile)]
            r = tiles[listed].astype(f32)
            e = (1.0 + confidence * r) * (r - mul(u, v, NT))
            e = jnp.where(s < live, e, 0.0).astype(bf16)
            slots_now.append((u_index, i_index, v, e))
        terms = [(a, b, mul(e, v, NN), mul(users_t[a], e, NN)) for a, b, v, e in slots_now]
        for a, b, to_user, to_item in terms:
            total[tile_rows(a, tile)] += to_user
            item_t[b] += to_item

    def step(g, carry):
        work(g * group, group)
        return carry

    whole = lax.div(live, group)
    left = live - whole * group
    whole = whole + (left > rests[-1]).astype(jnp.int32)
    lax.fori_loop(0, whole, step, 0)
    below = 0
    for size in rests:

        @pl.when((left > below) & (left <= size))
        def _(size=size):
            work(whole * group, size)

        below = size


class Tiles:
    def __init__(self, ratings, stop, counts, place, sems):
        self.ratings, self.stop, self.place, self.sems = ratings, stop, place, sems
        slots = ratings.shape[3] if counts is None else counts[stop]
        self.count = steps(slots, chunk)

    def copy(self, g):
        rows = pl.ds(g * chunk, chunk)
        return pltpu.make_async_copy(self.ratings.at[0, 0, self.stop, rows], self.place.at[rows], self.sems.at[g])

    def start(self):
        def begin(g, carry):
            self.copy(g).start()
            return carry

        lax.fori_loop(0, self.count, begin, 0)

    def wait(self):
        def finish(g, carry):
            self.copy(g).wait()
            return carry

        lax.fori_loop(0, self.count, finish, 0)


def own_kernel(
    counts, user_tiles, item_tiles, users, items, ratings,
    total, own_t, near_r, users_v, users_t, counts_v, ut_v, it_v,
    counts_s, ut_s, it_s, items_v, own_r, small, arrive,
):
    tile = ratings.shape[-1]
    core = lax.rem(lax.axis_index("rep"), cores)
    lists = [
        pltpu.make_async_copy(counts.at[0, 0], counts_s, small.at[0]),
        pltpu.make_async_copy(user_tiles.at[0], ut_s, small.at[1]),
        pltpu.make_async_copy(item_tiles.at[0], it_s, small.at[2]),
    ]
    blocks = [
        pltpu.make_async_copy(users, users_v, small.at[3]),
        pltpu.make_async_copy(items, items_v, small.at[4]),
        pltpu.make_async_copy(counts, counts_v, small.at[5]),
        pltpu.make_async_copy(user_tiles, ut_v, small.at[6]),
        pltpu.make_async_copy(item_tiles, it_v, small.at[7]),
    ]
    for copy in lists + blocks:
        copy.start()
    lists[0].wait()
    plans = [
        Tiles(ratings, 0, counts_s, own_r, arrive.at[0]),
        Tiles(ratings, near_stop(core), counts_s, near_r, arrive.at[1]),
    ]
    for plan in plans:
        plan.start()
    total[...] = jnp.zeros_like(total)
    own_t[...] = jnp.zeros_like(own_t)
    for copy in lists[1:] + blocks:
        copy.wait()
    for t in range(users_t.shape[0]):
        users_t[t] = users_v[pl.ds(t * tile, tile)].T
    plans[0].wait()
    run_slots(counts_s[0], 0, ut_s, it_s, users_v, users_t, items_v, own_r, total, own_t)
    plans[1].wait()


def own_call(counts, user_tiles, item_tiles, users, items, ratings):
    tile, slots, stops, rank = ratings.shape[-1], ratings.shape[3], ratings.shape[2], users.shape[1]
    n_user, n_item = users.shape[0] // tile, items.shape[0] // tile
    some_tiles = (-(-slots // group) * group, tile, tile)
    shape = jax.ShapeDtypeStruct
    return pl.pallas_call(
        own_kernel,
        out_shape=(
            shape(users.shape, f32),
            shape((n_item, rank, tile), f32),
            shape(some_tiles, ratings.dtype),
            shape(users.shape, users.dtype),
            shape((n_user, rank, tile), users.dtype),
            shape(counts.shape, counts.dtype),
            shape(user_tiles.shape, user_tiles.dtype),
            shape(item_tiles.shape, item_tiles.dtype),
        ),
        in_specs=[anywhere] * 6,
        out_specs=[vmem] * 8,
        scratch_shapes=[
            pltpu.SMEM((stops,), jnp.int32),
            pltpu.SMEM((stops, 1, slots), jnp.int32),
            pltpu.SMEM((stops, 1, slots), jnp.int32),
            pltpu.VMEM(items.shape, items.dtype),
            pltpu.VMEM(some_tiles, ratings.dtype),
            pltpu.SemaphoreType.DMA((8,)),
            pltpu.SemaphoreType.DMA((2, slots // chunk)),
        ],
        compiler_params=pltpu.CompilerParams(vmem_limit_bytes=8 * 2**20),
        cost_estimate=pl.CostEstimate(flops=10**10, bytes_accessed=8 * 10**6, transcendentals=0),
    )(*[pltpu.with_memory_space_constraint(a, pltpu.HBM) for a in (counts, user_tiles, item_tiles, users, items, ratings)])


def stop_kernel(which, following, *refs):
    counts_v, ut_v, it_v, users, users_t, block, tiles = refs[:7]
    refs = refs[8:]
    if following is not None:
        ratings, total, item_t, tiles_next, counts_s, ut_s, it_s, small, arrive = refs
    else:
        total, item_t, counts_s, ut_s, it_s, small = refs
    lists = [
        pltpu.make_async_copy(counts_v.at[0, 0], counts_s, small.at[0]),
        pltpu.make_async_copy(ut_v.at[0], ut_s, small.at[1]),
        pltpu.make_async_copy(it_v.at[0], it_s, small.at[2]),
    ]
    for copy in lists:
        copy.start()
    core = lax.rem(lax.axis_index("rep"), cores)
    if following is not None:
        plan = Tiles(ratings, following(core), None, tiles_next, arrive)
        plan.start()
    item_t[...] = jnp.zeros_like(item_t)
    for copy in lists:
        copy.wait()
    stop = which(core)
    run_slots(counts_s[stop], stop, ut_s, it_s, users, users_t, block, tiles, total, item_t)
    if following is not None:
        plan.wait()


def stop_call(which, lists, users, users_t, block, tiles, total, following=None, ratings=None):
    slots, tile = lists[1].shape[-1], tiles.shape[-1]
    stops = lists[0].shape[-1]
    operands = [*lists, users, users_t, block, tiles, total]
    out_shape = [
        jax.ShapeDtypeStruct(total.shape, f32),
        jax.ShapeDtypeStruct((block.shape[0] // tile, block.shape[1], tile), f32),
    ]
    scratch = [
        pltpu.SMEM((stops,), jnp.int32),
        pltpu.SMEM((stops, 1, slots), jnp.int32),
        pltpu.SMEM((stops, 1, slots), jnp.int32),
        pltpu.SemaphoreType.DMA((3,)),
    ]
    in_specs = [vmem] * len(operands)
    aliases = {len(operands) - 1: 0}
    if following is not None:
        operands.append(pltpu.with_memory_space_constraint(ratings, pltpu.HBM))
        in_specs.append(anywhere)
        out_shape.append(jax.ShapeDtypeStruct(tiles.shape, tiles.dtype))
        scratch.append(pltpu.SemaphoreType.DMA((slots // chunk,)))
    return pl.pallas_call(
        functools.partial(stop_kernel, which, following),
        out_shape=out_shape,
        in_specs=in_specs,
        out_specs=[vmem] * len(out_shape),
        input_output_aliases=aliases,
        scratch_shapes=scratch,
        compiler_params=pltpu.CompilerParams(vmem_limit_bytes=4 * 2**20),
        cost_estimate=pl.CostEstimate(flops=10**10, bytes_accessed=8 * 10**6, transcendentals=0),
    )(*operands)


def joint(block, target):
    n_blk, n_rep = lax.axis_size("blk"), lax.axis_size("rep")
    route = []
    for b in range(n_blk):
        for r in range(n_rep):
            to_b, to_r = target(b, r)
            route.append((b * n_rep + r, (to_b % n_blk) * n_rep + to_r))
    return lax.ppermute(block, ("blk", "rep"), route)


def swap(block, bit):
    return lax.ppermute(block, "rep", [(r, r ^ bit) for r in range(lax.axis_size("rep"))])


def on_device(users, items, ratings, user_tiles, item_tiles, counts):
    tile, slots, stops = ratings.shape[-1], ratings.shape[3], ratings.shape[2]
    n_rep = lax.axis_size("rep")
    core = lax.rem(lax.axis_index("rep"), cores)
    slot_cells = stops * slots * tile * tile
    rate_user = step_gain / math.sqrt(slot_cells / users.shape[0])
    rate_item = step_gain / math.sqrt(n_rep * slot_cells / items.shape[0])
    bound = cores * slots * tile * 2.0 * 3.0 * (4.0 + 4.0 * users.shape[1])
    scale = 2.0 ** math.floor(math.log2(60000.0 / bound))

    near = joint(items, lambda b, r: (b - near_stop(r % cores), r))
    user_tiles, item_tiles = (a.transpose(0, 2, 1, 3) for a in (user_tiles, item_tiles))
    total, own, near_r, users_v, users_t, *lists = own_call(
        counts, user_tiles, item_tiles, users, items, ratings
    )
    far = swap(near, 1)
    total, given, far_r = stop_call(near_stop, lists, users_v, users_t, near, near_r, total, far_stop, ratings)
    taken = swap((given * scale).astype(f16), 1).astype(f32) * (1.0 / scale)
    total, kept = stop_call(far_stop, lists, users_v, users_t, far, far_r, total)
    users32 = users_v.astype(f32)
    user_new = (users32 - rate_user * (total + shrinkage * users32)).astype(users.dtype)
    both = kept + taken
    half = both.shape[0] // cores

    def half_of(array, c):
        return lax.dynamic_slice_in_dim(array, c * half, half)

    straight = joint((half_of(both, core) * scale).astype(f16), lambda b, r: (b + far_stop(r % cores), r))
    across = joint((half_of(both, 1 - core) * scale).astype(f16), lambda b, r: (b + far_stop(r % cores), r ^ 1))
    own_half = half_of(own, core) + swap(half_of(own, 1 - core), 1)
    chip = own_half + (straight.astype(f32) + across.astype(f32)) * (1.0 / scale)
    bit = cores
    while bit < n_rep:
        coded = lax.optimization_barrier((chip * scale).astype(f16))
        chip = (coded.astype(f32) + swap(coded, bit).astype(f32)) * (1.0 / scale)
        bit *= 2
    chip = chip.transpose(0, 2, 1).reshape(-1, users.shape[1])
    rows = items.shape[0] // cores
    items32 = lax.dynamic_slice_in_dim(items, core * rows, rows).astype(f32)
    new_half = (items32 - rate_item * (chip + shrinkage * items32)).astype(items.dtype)
    other_half = swap(new_half, 1)
    low = jnp.where(core == 0, new_half, other_half)
    high = jnp.where(core == 0, other_half, new_half)
    return user_new, jnp.concatenate([low, high])


def solution(mesh):
    return jax.shard_map(
        on_device,
        mesh=mesh,
        in_specs=(
            P(("blk", "rep"), None),
            P("blk", None),
            P("blk", "rep", None, None, None, None),
            P("blk", "rep", None, None),
            P("blk", "rep", None, None),
            P("blk", "rep", None),
        ),
        out_specs=(P(("blk", "rep"), None), P("blk", None)),
        check_vma=False,
    )
```

```python
import functools
import math

import jax
import jax.numpy as jnp
from jax import lax
from jax.experimental import pallas as pl
from jax.experimental.pallas import tpu as pltpu
from jax.sharding import PartitionSpec as P

confidence = 0.5
shrinkage = 0.05
step_gain = 0.3
chunk = 8
group = 20
rests = (8, 12, 16)
cores = 2
f32, bf16, f16 = jnp.float32, jnp.bfloat16, jnp.float16

NT = (((1,), (1,)), ((), ()))
NN = (((1,), (0,)), ((), ()))
anywhere = pl.BlockSpec(memory_space=pl.ANY)
vmem = pl.BlockSpec(memory_space=pltpu.VMEM)


def mul(a, b, dims):
    return lax.dot_general(a, b, dims, preferred_element_type=f32)


def tile_rows(index, tile):
    return pl.ds(pl.multiple_of(index * tile, tile), tile)


def near_stop(core):
    return 1 + core


def far_stop(core):
    return 2 - core


def steps(live, size):
    return (live + size - 1) // size if isinstance(live, int) else lax.div(live + size - 1, size)


def run_slots(live, stop, ut_s, it_s, users, users_t, block, tiles, total, item_t):
    tile = tiles.shape[-1]

    def work(first, size):
        slots_now = []
        for k in range(size):
            s = first + k
            listed = jnp.minimum(s, ut_s.shape[-1] - 1)
            u_index = ut_s[stop, 0, listed]
            i_index = it_s[stop, 0, listed]
            u = users[tile_rows(u_index, tile)]
            v = block[tile_rows(i_index, tile)]
            r = tiles[listed].astype(f32)
            e = (1.0 + confidence * r) * (r - mul(u, v, NT))
            e = jnp.where(s < live, e, 0.0).astype(bf16)
            slots_now.append((u_index, i_index, v, e))
        terms = [(a, b, mul(e, v, NN), mul(users_t[a], e, NN)) for a, b, v, e in slots_now]
        for a, b, to_user, to_item in terms:
            total[tile_rows(a, tile)] += to_user
            item_t[b] += to_item

    def step(g, carry):
        work(g * group, group)
        return carry

    whole = lax.div(live, group)
    left = live - whole * group
    whole = whole + (left > rests[-1]).astype(jnp.int32)
    lax.fori_loop(0, whole, step, 0)
    below = 0
    for size in rests:

        @pl.when((left > below) & (left <= size))
        def _(size=size):
            work(whole * group, size)

        below = size


class Tiles:
    def __init__(self, ratings, stop, counts, place, sems):
        self.ratings, self.stop, self.place, self.sems = ratings, stop, place, sems
        slots = ratings.shape[3] if counts is None else counts[stop]
        self.count = steps(slots, chunk)

    def copy(self, g):
        rows = pl.ds(g * chunk, chunk)
        return pltpu.make_async_copy(self.ratings.at[0, 0, self.stop, rows], self.place.at[rows], self.sems.at[g])

    def start(self):
        def begin(g, carry):
            self.copy(g).start()
            return carry

        lax.fori_loop(0, self.count, begin, 0)

    def wait(self):
        def finish(g, carry):
            self.copy(g).wait()
            return carry

        lax.fori_loop(0, self.count, finish, 0)


def own_kernel(
    counts, user_tiles, item_tiles, users, items, ratings,
    total, own_t, near_r, users_v, users_t, counts_v, ut_v, it_v,
    counts_s, ut_s, it_s, items_v, own_r, small, arrive,
):
    tile = ratings.shape[-1]
    core = lax.rem(lax.axis_index("rep"), cores)
    lists = [
        pltpu.make_async_copy(counts.at[0, 0], counts_s, small.at[0]),
        pltpu.make_async_copy(user_tiles.at[0], ut_s, small.at[1]),
        pltpu.make_async_copy(item_tiles.at[0], it_s, small.at[2]),
    ]
    blocks = [
        pltpu.make_async_copy(users, users_v, small.at[3]),
        pltpu.make_async_copy(items, items_v, small.at[4]),
        pltpu.make_async_copy(counts, counts_v, small.at[5]),
        pltpu.make_async_copy(user_tiles, ut_v, small.at[6]),
        pltpu.make_async_copy(item_tiles, it_v, small.at[7]),
    ]
    for copy in lists + blocks:
        copy.start()
    lists[0].wait()
    plans = [
        Tiles(ratings, 0, counts_s, own_r, arrive.at[0]),
        Tiles(ratings, near_stop(core), counts_s, near_r, arrive.at[1]),
    ]
    for plan in plans:
        plan.start()
    total[...] = jnp.zeros_like(total)
    own_t[...] = jnp.zeros_like(own_t)
    for copy in lists[1:] + blocks:
        copy.wait()
    for t in range(users_t.shape[0]):
        users_t[t] = users_v[pl.ds(t * tile, tile)].T
    plans[0].wait()
    run_slots(counts_s[0], 0, ut_s, it_s, users_v, users_t, items_v, own_r, total, own_t)
    plans[1].wait()


def own_call(counts, user_tiles, item_tiles, users, items, ratings):
    tile, slots, stops, rank = ratings.shape[-1], ratings.shape[3], ratings.shape[2], users.shape[1]
    n_user, n_item = users.shape[0] // tile, items.shape[0] // tile
    some_tiles = (-(-slots // group) * group, tile, tile)
    shape = jax.ShapeDtypeStruct
    return pl.pallas_call(
        own_kernel,
        out_shape=(
            shape(users.shape, f32),
            shape((n_item, rank, tile), f32),
            shape(some_tiles, ratings.dtype),
            shape(users.shape, users.dtype),
            shape((n_user, rank, tile), users.dtype),
            shape(counts.shape, counts.dtype),
            shape(user_tiles.shape, user_tiles.dtype),
            shape(item_tiles.shape, item_tiles.dtype),
        ),
        in_specs=[anywhere] * 6,
        out_specs=[vmem] * 8,
        scratch_shapes=[
            pltpu.SMEM((stops,), jnp.int32),
            pltpu.SMEM((stops, 1, slots), jnp.int32),
            pltpu.SMEM((stops, 1, slots), jnp.int32),
            pltpu.VMEM(items.shape, items.dtype),
            pltpu.VMEM(some_tiles, ratings.dtype),
            pltpu.SemaphoreType.DMA((8,)),
            pltpu.SemaphoreType.DMA((2, slots // chunk)),
        ],
        compiler_params=pltpu.CompilerParams(vmem_limit_bytes=8 * 2**20),
        cost_estimate=pl.CostEstimate(flops=10**10, bytes_accessed=8 * 10**6, transcendentals=0),
    )(*[pltpu.with_memory_space_constraint(a, pltpu.HBM) for a in (counts, user_tiles, item_tiles, users, items, ratings)])


def stop_kernel(which, following, *refs):
    counts_v, ut_v, it_v, users, users_t, block, tiles = refs[:7]
    refs = refs[8:]
    if following is not None:
        ratings, total, item_t, tiles_next, counts_s, ut_s, it_s, small, arrive = refs
    else:
        total, item_t, counts_s, ut_s, it_s, small = refs
    lists = [
        pltpu.make_async_copy(counts_v.at[0, 0], counts_s, small.at[0]),
        pltpu.make_async_copy(ut_v.at[0], ut_s, small.at[1]),
        pltpu.make_async_copy(it_v.at[0], it_s, small.at[2]),
    ]
    for copy in lists:
        copy.start()
    core = lax.rem(lax.axis_index("rep"), cores)
    if following is not None:
        plan = Tiles(ratings, following(core), None, tiles_next, arrive)
        plan.start()
    item_t[...] = jnp.zeros_like(item_t)
    for copy in lists:
        copy.wait()
    stop = which(core)
    run_slots(counts_s[stop], stop, ut_s, it_s, users, users_t, block, tiles, total, item_t)
    if following is not None:
        plan.wait()


def stop_call(which, lists, users, users_t, block, tiles, total, following=None, ratings=None):
    slots, tile = lists[1].shape[-1], tiles.shape[-1]
    stops = lists[0].shape[-1]
    operands = [*lists, users, users_t, block, tiles, total]
    out_shape = [
        jax.ShapeDtypeStruct(total.shape, f32),
        jax.ShapeDtypeStruct((block.shape[0] // tile, block.shape[1], tile), f32),
    ]
    scratch = [
        pltpu.SMEM((stops,), jnp.int32),
        pltpu.SMEM((stops, 1, slots), jnp.int32),
        pltpu.SMEM((stops, 1, slots), jnp.int32),
        pltpu.SemaphoreType.DMA((3,)),
    ]
    in_specs = [vmem] * len(operands)
    aliases = {len(operands) - 1: 0}
    if following is not None:
        operands.append(pltpu.with_memory_space_constraint(ratings, pltpu.HBM))
        in_specs.append(anywhere)
        out_shape.append(jax.ShapeDtypeStruct(tiles.shape, tiles.dtype))
        scratch.append(pltpu.SemaphoreType.DMA((slots // chunk,)))
    return pl.pallas_call(
        functools.partial(stop_kernel, which, following),
        out_shape=out_shape,
        in_specs=in_specs,
        out_specs=[vmem] * len(out_shape),
        input_output_aliases=aliases,
        scratch_shapes=scratch,
        compiler_params=pltpu.CompilerParams(vmem_limit_bytes=4 * 2**20),
        cost_estimate=pl.CostEstimate(flops=10**10, bytes_accessed=8 * 10**6, transcendentals=0),
    )(*operands)


def joint(block, target):
    n_blk, n_rep = lax.axis_size("blk"), lax.axis_size("rep")
    route = []
    for b in range(n_blk):
        for r in range(n_rep):
            to_b, to_r = target(b, r)
            route.append((b * n_rep + r, (to_b % n_blk) * n_rep + to_r))
    return lax.ppermute(block, ("blk", "rep"), route)


def swap(block, bit):
    return lax.ppermute(block, "rep", [(r, r ^ bit) for r in range(lax.axis_size("rep"))])


def on_device(users, items, ratings, user_tiles, item_tiles, counts):
    tile, slots, stops = ratings.shape[-1], ratings.shape[3], ratings.shape[2]
    n_rep = lax.axis_size("rep")
    core = lax.rem(lax.axis_index("rep"), cores)
    slot_cells = stops * slots * tile * tile
    rate_user = step_gain / math.sqrt(slot_cells / users.shape[0])
    rate_item = step_gain / math.sqrt(n_rep * slot_cells / items.shape[0])
    bound = cores * slots * tile * 2.0 * 3.0 * (4.0 + 4.0 * users.shape[1])
    scale = 2.0 ** math.floor(math.log2(60000.0 / bound))

    near = joint(items, lambda b, r: (b - near_stop(r % cores), r))
    user_tiles, item_tiles = (a.transpose(0, 2, 1, 3) for a in (user_tiles, item_tiles))
    total, own, near_r, users_v, users_t, *lists = own_call(
        counts, user_tiles, item_tiles, users, items, ratings
    )
    far = swap(near, 1)
    total, given, far_r = stop_call(near_stop, lists, users_v, users_t, near, near_r, total, far_stop, ratings)
    taken = swap((given * scale).astype(f16), 1).astype(f32) * (1.0 / scale)
    total, kept = stop_call(far_stop, lists, users_v, users_t, far, far_r, total)
    users32 = users_v.astype(f32)
    user_new = (users32 - rate_user * (total + shrinkage * users32)).astype(users.dtype)
    both = kept + taken
    half = both.shape[0] // cores

    def half_of(array, c):
        return lax.dynamic_slice_in_dim(array, c * half, half)

    straight = joint((half_of(both, core) * scale).astype(f16), lambda b, r: (b + far_stop(r % cores), r))
    across = joint((half_of(both, 1 - core) * scale).astype(f16), lambda b, r: (b + far_stop(r % cores), r ^ 1))
    own_half = half_of(own, core) + swap(half_of(own, 1 - core), 1)
    chip = own_half + (straight.astype(f32) + across.astype(f32)) * (1.0 / scale)
    bit = cores
    while bit < n_rep:
        coded = lax.optimization_barrier((chip * scale).astype(f16))
        chip = (coded.astype(f32) + swap(coded, bit).astype(f32)) * (1.0 / scale)
        bit *= 2
    chip = chip.transpose(0, 2, 1).reshape(-1, users.shape[1])
    rows = items.shape[0] // cores
    items32 = lax.dynamic_slice_in_dim(items, core * rows, rows).astype(f32)
    new_half = (items32 - rate_item * (chip + shrinkage * items32)).astype(items.dtype)
    other_half = swap(new_half, 1)
    low = jnp.where(core == 0, new_half, other_half)
    high = jnp.where(core == 0, other_half, new_half)
    return user_new, jnp.concatenate([low, high])


def solution(mesh):
    return jax.shard_map(
        on_device,
        mesh=mesh,
        in_specs=(
            P(("blk", "rep"), None),
            P("blk", None),
            P("blk", "rep", None, None, None, None),
            P("blk", "rep", None, None),
            P("blk", "rep", None, None),
            P("blk", "rep", None),
        ),
        out_specs=(P(("blk", "rep"), None), P("blk", None)),
        check_vma=False,
    )
```
